32 devices in a mesh: dp: 8 (over z, x), row: 2 (over y), col: 2 (over core).
Axes of the slice: x: 2, y: 2, z: 4, core: 2. Of those that a mesh axis runs over, the one named last changes fastest.
Arguments:
- block_in: bfloat16 [96, 169344], P(('dp', 'row', 'col')), may hold values from -6 to 6
- out_grad: bfloat16 [96, 169344], P(('dp', 'row', 'col')), may hold values from -6 to 6
- width_mask: int32 [4, 216], replicated, may hold values from 0 to 1, as said below
- head_mask: int32 [4, 12], replicated, may hold values from 0 to 1, as said below
- hidden_mask: int32 [4, 864], replicated, may hold values from 0 to 1, as said below
- qkv_weight: bfloat16 [216, 648], P('row', 'col'), may hold values from -0.4375 to 0.4375
- proj_weight: bfloat16 [216, 216], P('row', 'col'), may hold values from -1.5 to 1.5
- fc1_weight: bfloat16 [216, 864], P('row', 'col'), may hold values from -0.4375 to 0.4375
- fc2_weight: bfloat16 [864, 216], P('row', 'col'), may hold values from -0.4375 to 0.4375
- norm1_gain: float32 [216], replicated, may hold values from 0.1 to 1.9
- norm1_shift: float32 [216], replicated, may hold values from -1.75 to 1.75
- proj_bias: float32 [216], replicated, may hold values from -1.75 to 1.75
- norm2_gain: float32 [216], replicated, may hold values from 0.1 to 1.9
- second_norm_bias: float32 [216], replicated, may hold values from -1.75 to 1.75
- conv_taps: float32 [9, 864], replicated, may hold values from -2 to 2
- bn_gain: float32 [864], replicated, may hold values from 0.1 to 1.9
- bn_shift: float32 [864], replicated, may hold values from -3 to 3
- output_bias: float32 [216], replicated, may hold values from -1.75 to 1.75
- talk_mix: float32 [12, 12], replicated, may hold values from -3.5 to 3.5
Outputs:
- block_out: float32 [96, 169344], P(('dp', 'row', 'col'))
- in_grad: float32 [96, 169344], P(('dp', 'row', 'col'))
- qkv_grad: float32 [216, 648], P('row', 'col')
- proj_grad: float32 [216, 216], P('row', 'col')
- fc1_grad: float32 [216, 864], P('row', 'col')
- fc2_grad: float32 [864, 216], P('row', 'col')
- norm1_gain_grad: float32 [216], replicated
- norm1_shift_grad: float32 [216], replicated
- proj_bias_grad: float32 [216], replicated
- norm2_gain_grad: float32 [216], replicated
- norm2_shift_grad: float32 [216], replicated
- taps_grad: float32 [9, 864], replicated
- bn_gain_grad: float32 [864], replicated
- bn_shift_grad: float32 [864], replicated
- out_bias_grad: float32 [216], replicated
- talk_grad: float32 [12, 12], replicated
- bn_mean: float32 [4, 864], replicated
- bn_var: float32 [4, 864], replicated
The draws below stay inside these ranges and needn't reach their ends.
Inputs may be any that keep to these rules, and one draw needn't show every extreme that they name: `width_mask`: row s is 1 on its first k_s channels and 0 after them, k_s an integer from 216 - 2 * (24) to 216. Row 0 has k = 216, row 1 k = 168; rows 2 and 3 are drawn. `head_mask`: row s is 1 on its first c_s heads, c_s one of 8, 10, 12. Row 0 has the most, row 1 the fewest. `hidden_mask`: row s is 1 on its first r_s * k_s units, k_s the active width of the same row of width_mask and r_s one of 2, 3, 4. Row 0 has r = 4, row 1 r = 2.
All inputs are finite; a program needn't handle non-finite values.
Results may differ from the reference program's by a relative error of at most 0.02.
Values may be sent and summed in bfloat16 or wider, within the bound.
No kernel may reach another device: no remote copies, remote signals or barrier semaphores. Data moves between devices by JAX's collectives and lax.ppermute only.
A program may use at most 320 MiB of HBM per device.

```python
import math
import jax
import jax.numpy as jnp
from jax import lax

H = 12
E = 18
GRID = 14
SUBNETS = 4
D = 216
FF = 864
L = 196
IMAGES = 96


def subnet_picks(key):
    member_ids = jnp.arange(SUBNETS)
    span = 2 * (D // 9)
    width_off = jax.random.randint(jax.random.fold_in(key, 11), (SUBNETS,), 0, span + 1)
    width_off = jnp.where(member_ids == 0, span, jnp.where(member_ids == 1, 0, width_off))
    head_pick = jax.random.randint(jax.random.fold_in(key, 12), (SUBNETS,), 0, 3)
    head_pick = jnp.where(member_ids == 0, 2, jnp.where(member_ids == 1, 0, head_pick))
    ratio_pick = jax.random.randint(jax.random.fold_in(key, 13), (SUBNETS,), 0, 3)
    ratio_pick = jnp.where(member_ids == 0, 2, jnp.where(member_ids == 1, 0, ratio_pick))
    return (width_off.astype(jnp.int32), head_pick.astype(jnp.int32), ratio_pick.astype(jnp.int32))


def width_counts(picks):
    return D - 2 * (D // 9) + picks[0]


def draw_width_mask(key, part):
    picks = subnet_picks(key)
    return (jnp.arange(D)[None, :] < width_counts(picks)[:, None]).astype(jnp.int32)


def draw_head_mask(key, part):
    picks = subnet_picks(key)
    counts_h = H - (2 - picks[1]) * (H // 6)
    return (jnp.arange(H)[None, :] < counts_h[:, None]).astype(jnp.int32)


def draw_hidden_mask(key, part):
    picks = subnet_picks(key)
    counts_e = (2 + picks[2]) * width_counts(picks)
    return (jnp.arange(FF)[None, :] < counts_e[:, None]).astype(jnp.int32)


def levels(stream_key, dims, pieces, least, largest):
    level = 1.0
    for dim, shards_of in pieces:
        draws = jax.random.uniform(jax.random.fold_in(jax.random.fold_in(stream_key, 6), dim), (shards_of,), jnp.float32, least / len(pieces), largest / len(pieces))
        level = level * jnp.repeat(jnp.exp(draws), dims[dim] // shards_of).reshape((-1,) + (1,) * (len(dims) - 1 - dim))
    return level


def noise(stream_key, extent, spread, limit, pieces=(), held_as=jnp.bfloat16):
    drawn = jax.random.normal(stream_key, extent, jnp.float32) * spread
    if len(pieces) > 0:
        drawn = levels(stream_key, extent, pieces, -0.22, 0.18) * drawn
    return jnp.clip(drawn, min=-limit, max=limit).astype(held_as)


def setup_inputs(seed: int = 0) -> dict:
    splits = jax.random.split(jax.random.key(seed), 20)
    block_in = noise(splits[0], (IMAGES, SUBNETS * L * D), 1.0, 6.0, ((0, 32),))
    out_grad = noise(splits[1], (IMAGES, SUBNETS * L * D), 1.0, 6.0, ((0, 32),))
    width_mask = draw_width_mask(jax.random.fold_in(splits[19], 71), 0)
    head_mask = draw_head_mask(jax.random.fold_in(splits[19], 71), 0)
    hidden_mask = draw_hidden_mask(jax.random.fold_in(splits[19], 71), 0)
    qkv_weight = noise(splits[5], (D, 3 * D), D ** -0.5, 0.4375, ((0, 2), (1, 2)))
    proj_weight = noise(splits[6], (D, D), (D // 12) ** -0.5, 1.5, ((0, 2), (1, 2)))
    fc1_weight = noise(splits[7], (D, FF), D ** -0.5, 0.4375, ((0, 2), (1, 2)))
    fc2_weight = noise(splits[8], (FF, D), (FF // 4) ** -0.5, 0.4375, ((0, 2), (1, 2)))
    norm1_gain = jnp.clip(1.0 + 0.18 * jax.random.normal(splits[9], (D,), jnp.float32), 0.1, 1.9)
    norm1_shift = noise(splits[10], (D,), 0.3, 1.75, (), jnp.float32)
    proj_bias = noise(splits[11], (D,), 0.3, 1.75, (), jnp.float32)
    norm2_gain = jnp.clip(1.0 + 0.18 * jax.random.normal(splits[12], (D,), jnp.float32), 0.1, 1.9)
    second_norm_bias = noise(splits[13], (D,), 0.3, 1.75, (), jnp.float32)
    conv_taps = noise(splits[14], (9, FF), 9 ** -0.5, 2.0, (), jnp.float32)
    bn_gain = jnp.clip(1.0 + 0.18 * jax.random.normal(splits[15], (FF,), jnp.float32), 0.1, 1.9)
    bn_shift = noise(splits[16], (FF,), 0.5, 3.0, (), jnp.float32)
    output_bias = noise(splits[17], (D,), 0.3, 1.75, (), jnp.float32)
    talk_mix = noise(splits[18], (H, H), 0.6, 3.5, (), jnp.float32)
    return {"block_in": block_in, "out_grad": out_grad, "width_mask": width_mask, "head_mask": head_mask, "hidden_mask": hidden_mask, "qkv_weight": qkv_weight, "proj_weight": proj_weight, "fc1_weight": fc1_weight, "fc2_weight": fc2_weight, "norm1_gain": norm1_gain, "norm1_shift": norm1_shift, "proj_bias": proj_bias, "norm2_gain": norm2_gain, "second_norm_bias": second_norm_bias, "conv_taps": conv_taps, "bn_gain": bn_gain, "bn_shift": bn_shift, "output_bias": output_bias, "talk_mix": talk_mix}


@jax.custom_vjp
def low(v):
    return lax.optimization_barrier(v.astype(jnp.bfloat16)).astype(jnp.float32)

@jax.custom_vjp
def low_back(v):
    return v

def low_keep(v):
    return (low(v), None)

def low_pass(kept, grad):
    return (grad,)

def back_keep(v):
    return (v, None)

def back_low(kept, grad):
    return (low(grad),)
low.defvjp(low_keep, low_pass)
low_back.defvjp(back_keep, back_low)
norm_eps = 1e-05
highest = lax.Precision.HIGHEST

def layer_norm(values, gain, shift, keep, active):
    mean_val = lax.optimization_barrier(jnp.sum(values * keep, axis=-1, keepdims=True)) / active
    centred = (values - mean_val) * keep
    var_val = lax.optimization_barrier(jnp.sum(centred * centred, axis=-1, keepdims=True)) / active
    return centred * lax.rsqrt(var_val + norm_eps) * gain + shift * keep

def depthwise(grid, taps):
    grid_rows, grid_cols = (grid.shape[-3], grid.shape[-2])
    widths = [(0, 0)] * (grid.ndim - 3) + [(1, 1), (1, 1), (0, 0)]
    padded = jnp.pad(grid, widths)
    result = jnp.zeros(grid.shape, jnp.float32)
    for vert in range(3):
        for horiz in range(3):
            result = result + taps[3 * vert + horiz] * padded[..., vert:vert + grid_rows, horiz:horiz + grid_cols, :]
    return result

def attend_group(queries, keys_all, values_all, mix, head_keep):
    head_scale = 1.0 / math.sqrt(queries.shape[-1])
    scores = low_back(jnp.einsum('blhe,bmhe->bhlm', queries, keys_all, precision=highest) * head_scale)
    mixed = jnp.einsum('hg,bglm->bhlm', mix, scores, precision=highest)
    probs = low(jax.nn.softmax(mixed, axis=-1))
    return jnp.einsum('bhlm,bmhe->blhe', probs, values_all, precision=highest) * head_keep[None, None, :, None]

def subnet_forward(inputs, qkv_weight, proj_weight, fc1_weight, fc2_weight, norm1_gain, norm1_shift, proj_bias, norm2_gain, second_norm_bias, conv_taps, bn_gain, bn_shift, output_bias, talk_mix, keep_w, keep_h, keep_e):
    images = inputs.shape[0]
    token_rows = inputs.reshape(images * L, D)
    active = jnp.sum(keep_w)
    norm_one = low(layer_norm(token_rows, norm1_gain, norm1_shift, keep_w, active))
    packed = low(low_back(jnp.dot(norm_one, qkv_weight, precision=highest)))
    group = math.gcd(images, 16)
    packed = packed.reshape(images // group, group, L, 3, H, E)
    mix = talk_mix * keep_h[None, :]

    def attend_one(operands):
        return attend_group(operands[0], operands[1], operands[2], mix, keep_h)
    attended = lax.map(jax.checkpoint(attend_one), (packed[:, :, :, 0], packed[:, :, :, 1], packed[:, :, :, 2]))
    attended = low(low_back(attended.reshape(images * L, D)))
    residual_one = token_rows + low_back(jnp.dot(attended, proj_weight, precision=highest) + proj_bias) * keep_w
    norm_two = low(layer_norm(residual_one, norm2_gain, second_norm_bias, keep_w, active))
    hidden = low_back(jnp.dot(norm_two, fc1_weight, precision=highest)) * keep_e
    conv_out = depthwise(hidden.reshape(images, GRID, GRID, FF), conv_taps)
    bn_mean = lax.optimization_barrier(jnp.mean(conv_out, axis=(0, 1, 2)))
    bn_var = lax.optimization_barrier(jnp.mean(conv_out * conv_out, axis=(0, 1, 2))) - bn_mean * bn_mean
    normed = (conv_out - bn_mean) * lax.rsqrt(bn_var + norm_eps) * bn_gain + bn_shift
    swished = low((normed * jax.nn.sigmoid(normed) * keep_e).reshape(images * L, FF))
    block_out = residual_one + low_back(jnp.dot(swished, fc2_weight, precision=highest) + output_bias) * keep_w
    return (block_out.reshape(inputs.shape), (bn_mean, bn_var))

def reference(block_in, out_grad, width_mask, head_mask, hidden_mask, qkv_weight, proj_weight, fc1_weight, fc2_weight, norm1_gain, norm1_shift, proj_bias, norm2_gain, second_norm_bias, conv_taps, bn_gain, bn_shift, output_bias, talk_mix):
    params = tuple((weight.astype(jnp.float32) for weight in (qkv_weight, proj_weight, fc1_weight, fc2_weight, norm1_gain, norm1_shift, proj_bias, norm2_gain, second_norm_bias, conv_taps, bn_gain, bn_shift, output_bias, talk_mix)))
    inputs_all = block_in.reshape(IMAGES, SUBNETS, L, D)
    grads_all = out_grad.reshape(IMAGES, SUBNETS, L, D)
    outputs, in_grads, means, variances = ([], [], [], [])
    totals = None
    for member in range(SUBNETS):
        keep_w = width_mask[member].astype(jnp.float32)
        keep_h = head_mask[member].astype(jnp.float32)
        keep_e = hidden_mask[member].astype(jnp.float32)

        def forward(inputs, *weights):
            return subnet_forward(inputs, *weights, keep_w, keep_h, keep_e)
        result, pullback, stats = jax.vjp(forward, inputs_all[:, member].astype(jnp.float32), *params, has_aux=True)
        grads = pullback(grads_all[:, member].astype(jnp.float32))
        outputs.append(result)
        in_grads.append(grads[0])
        means.append(stats[0])
        variances.append(stats[1])
        if totals is None:
            totals = list(grads[1:])
        else:
            totals = [left + right for left, right in zip(totals, grads[1:])]
    block_out = jnp.stack(outputs, axis=1).reshape(IMAGES, SUBNETS * L * D)
    in_grad = jnp.stack(in_grads, axis=1).reshape(IMAGES, SUBNETS * L * D)
    return (block_out, in_grad, totals[0], totals[1], totals[2], totals[3], totals[4], totals[5], totals[6], totals[7], totals[8], totals[9], totals[10], totals[11], totals[12], totals[13], jnp.stack(means), jnp.stack(variances))
```

```python
import functools
import math

import jax
import jax.numpy as jnp
import numpy as np
from jax import lax
from jax.experimental import pallas as pl
from jax.experimental.pallas import tpu as pltpu
from jax.sharding import PartitionSpec as P

H = 12
E = 18
GRID = 14
SUBNETS = 4
D = 216
FF = 864
L = 196

COLS = 16
LP = GRID * COLS
CP = 224
EP = 32
VP = H * EP
FP = 896
CHUNK = 256
CHUNKS = tuple((start, min(CHUNK, FP - start)) for start in range(0, FP, CHUNK))
HALO = COLS + LP + COLS
EDGE = 8
MIB = 1 << 20
Q_ROWS, K_ROWS, V_ROWS = slice(0, CP), slice(256, 256 + CP), slice(512, 512 + VP)
WP = 896

norm_eps = 1e-05
f32 = jnp.float32
bf16 = jnp.bfloat16
AXES = ("dp", "row", "col")
HEAD_SCALE = 1.0 / math.sqrt(E)
LOG2E = math.log2(math.e)


def dot_nn(a, b):
    return lax.dot_general(a, b, (((1,), (0,)), ((), ())), preferred_element_type=f32)


def dot_nt(a, b):
    return lax.dot_general(a, b, (((1,), (1,)), ((), ())), preferred_element_type=f32)


def token_rows(rows):
    return (lax.broadcasted_iota(jnp.int32, (rows, 1), 0) % COLS < GRID).astype(f32)


def norm_forward(values, keep, inv_active):
    mean_val = jnp.sum(values * keep, axis=-1, keepdims=True) * inv_active
    centred = (values - mean_val) * keep
    var_val = jnp.sum(centred * centred, axis=-1, keepdims=True) * inv_active
    inv_std = lax.rsqrt(var_val + norm_eps)
    return centred * inv_std, inv_std


def norm_backward(upstream, scaled, inv_std, gain, keep, inv_active):
    scaled_grad = upstream * gain
    first = jnp.sum(scaled_grad * keep, axis=-1, keepdims=True) * inv_active
    second = jnp.sum(scaled_grad * scaled, axis=-1, keepdims=True) * inv_active
    return keep * inv_std * (scaled_grad - first - scaled * second)


def rows_sum(v):
    return jnp.sum(v, axis=0, keepdims=True)


def attend_kernel(
    images, counts, actives, x_ref, kw_ref, g1_ref, b1_ref, wt_ref, w_ref, mix_ref, proj_ref, pb_ref,
    e_ref, inv_ref, att_ref, res_ref, qt_s, k_s, vt_s,
):
    member = pl.program_id(0)
    heads = counts[member, 0]
    inv_active = actives[member, 0]
    rows = images * LP
    keep = kw_ref[0]
    tokens = token_rows(LP)
    x = x_ref[:, 0].reshape(rows, D).astype(f32)
    scaled, _ = norm_forward(x, keep, inv_active)
    norm_one = (scaled * g1_ref[...] + b1_ref[...] * keep).astype(bf16)

    ones_row = (lax.broadcasted_iota(jnp.int32, (CP, 1), 0) == D).astype(f32)
    mask_lane = (lax.broadcasted_iota(jnp.int32, (1, CP), 1) == D).astype(f32)
    sum_rows = (lax.broadcasted_iota(jnp.int32, (VP, 1), 0) % EP == E).astype(f32)
    key_mask = (1.0 - tokens) * (-1e30) * mask_lane
    for i in range(images):
        mine = norm_one[i * LP : (i + 1) * LP]
        qt_s[i] = (dot_nt(wt_ref[Q_ROWS, :], mine) + ones_row).astype(bf16)
        k_s[i] = dot_nn(mine, w_ref[:, K_ROWS]).astype(bf16).astype(f32) + key_mask
        vt_s[i] = (dot_nt(wt_ref[V_ROWS, :], mine) + sum_rows).astype(bf16)
    att_ref[...] = jnp.zeros_like(att_ref)

    def one_pair(pair, carry):
        for offset in range(2):
            h = 2 * pair + offset
            mix_row = mix_ref[0, pl.ds(h, 1), :]
            for i in range(images):
                keys = (k_s[i] * mix_row).astype(bf16)
                mixed = dot_nn(keys, qt_s[i])
                peak = jnp.max(mixed, axis=0, keepdims=True)
                e = jnp.exp2((mixed - peak).astype(bf16))
                e_ref[0, i, h] = e
                out = dot_nn(vt_s[i, pl.ds(pl.multiple_of(h * EP, EP), EP), :], e)
                inv = 1.0 / out[E : E + 1]
                inv_ref[0, i, pl.ds(h, 1), :] = inv
                att_ref[0, i, pl.ds(pl.multiple_of(h * EP, EP), EP), :] = out * inv
        return carry

    lax.fori_loop(0, heads // 2, one_pair, 0)

    parts = []
    for i in range(images):
        attended = att_ref[0, i].astype(bf16).T
        parts.append(dot_nn(attended, proj_ref[...]))
    residual = x + keep * (jnp.concatenate(parts, axis=0) + pb_ref[...])
    res_ref[0] = residual


def hidden_kernel(
    images, counts, actives, res_ref, kw_ref, ke_ref, g2_ref, b2_ref, fc1_ref, taps_ref,
    hid_ref, conv_ref, sums_ref, halo_s,
):
    member = pl.program_id(0)
    hidden_count = counts[member, 1]
    inv_active = actives[member, 0]
    rows = images * LP
    keep = kw_ref[0]
    tokens = token_rows(LP)
    scaled, _ = norm_forward(res_ref[0], keep, inv_active)
    tokens_all = token_rows(rows)
    norm_two = ((scaled * g2_ref[...] + b2_ref[...] * keep) * tokens_all).astype(bf16)

    sums_ref[...] = jnp.zeros_like(sums_ref)

    @pl.when(member == 0)
    def _():
        halo_s[...] = jnp.zeros_like(halo_s)

    for start, width in CHUNKS:

        @pl.when(hidden_count > start)
        def _(start=start, width=width):
            weight = fc1_ref[:, start : start + width] * ke_ref[0, :, start : start + width]
            hidden = dot_nn(norm_two, weight)
            hid_ref[0, :, start : start + width] = hidden.astype(bf16)
            for half in range(width // 128):
                low = start + half * 128
                total = jnp.zeros((1, 128), f32)
                total_square = jnp.zeros((1, 128), f32)
                for i in range(images):
                    base = EDGE + i * HALO + COLS
                    halo_s[half, base : base + LP, :] = hidden[
                        i * LP : (i + 1) * LP, half * 128 : half * 128 + 128
                    ]
                    acc = jnp.zeros((LP, 128), f32)
                    for a in range(3):
                        for b in range(3):
                            first = base + (a - 1) * COLS + b - 1
                            tap = taps_ref[3 * a + b : 3 * a + b + 1, low : low + 128]
                            acc = acc + tap * halo_s[half, first : first + LP, :]
                    conv_ref[0, i * LP : (i + 1) * LP, low : low + 128] = acc
                    valid = acc * tokens
                    total = total + rows_sum(valid)
                    total_square = total_square + rows_sum(valid * acc)
                sums_ref[0, 0:1, low : low + 128] = total
                sums_ref[0, 1:2, low : low + 128] = total_square


def batch_stats(totals, tokens_all):
    mean_val = totals[0:1] * (1.0 / tokens_all)
    var_val = totals[1:2] * (1.0 / tokens_all) - mean_val * mean_val
    return mean_val, var_val


def middle_kernel(
    images, tokens_all, counts, conv_ref, res_ref, og_ref, kw_ref, ke_ref, fc2_ref, ob_ref, gain_ref, shift_ref,
    totals_ref, out_ref, ng_ref, sums_ref, fc2g_ref, obg_ref, mean_ref, var_ref, acc_s,
):
    member = pl.program_id(0)
    hidden_count = counts[member, 1]
    rows = images * LP
    keep = kw_ref[0]
    out_low = (og_ref[:, 0].reshape(rows, D).astype(f32) * keep).astype(bf16)
    out_low_t = out_low.T

    @pl.when(member == 0)
    def _():
        fc2g_ref[...] = jnp.zeros_like(fc2g_ref)
        obg_ref[...] = jnp.zeros_like(obg_ref)

    obg_ref[...] += rows_sum(out_low.astype(f32))
    sums_ref[...] = jnp.zeros_like(sums_ref)
    mean_all, var_all = batch_stats(totals_ref[0], tokens_all)
    mean_ref[0] = mean_all
    var_ref[0] = var_all
    acc_s[...] = jnp.zeros_like(acc_s)
    for start, width in CHUNKS:

        @pl.when(hidden_count > start)
        def _(start=start, width=width):
            span = slice(start, start + width)
            mean_val, var_val = batch_stats(totals_ref[0, :, span], tokens_all)
            centred = (conv_ref[0, :, span] - mean_val) * lax.rsqrt(var_val + norm_eps)
            normed = centred * gain_ref[:, span] + shift_ref[:, span]
            gate = jax.nn.sigmoid(normed)
            kept_gate = gate * ke_ref[0, :, span].astype(f32)
            swished = (normed * kept_gate).astype(bf16)
            weight = fc2_ref[span, :]
            acc_s[...] += dot_nn(swished, weight)
            fc2g_ref[:, span] += dot_nn(out_low_t, swished)
            swish_grad = dot_nt(out_low, weight)
            normed_grad = swish_grad * kept_gate * (1.0 + normed * (1.0 - gate))
            ng_ref[0, :, span] = normed_grad
            sums_ref[0, 0:1, span] = rows_sum(normed_grad)
            sums_ref[0, 1:2, span] = rows_sum(normed_grad * centred)

    result = res_ref[0] + keep * (acc_s[...] + ob_ref[...])
    out_ref[:, 0] = result.reshape(images, LP, D)


def hidden_back_kernel(
    images, tokens_all, counts, actives, og_ref, res_ref, hid_ref, conv_ref, ng_ref, kw_ref, g2_ref, b2_ref,
    fc1_ref, taps_ref, gain_ref, totals_ref, totals2_ref,
    resg_ref, fc1g_ref, tapsg_ref, small_ref, halo_s, acc_s,
):
    member = pl.program_id(0)
    hidden_count = counts[member, 1]
    inv_active = actives[member, 0]
    rows = images * LP
    keep = kw_ref[0]
    tokens = token_rows(LP)
    tokens_rows = token_rows(rows)

    @pl.when(member == 0)
    def _():
        halo_s[...] = jnp.zeros_like(halo_s)
        for ref in (fc1g_ref, tapsg_ref, small_ref):
            ref[...] = jnp.zeros_like(ref)

    scaled_two, inv_two = norm_forward(res_ref[0], keep, inv_active)
    norm_two = ((scaled_two * g2_ref[...] + b2_ref[...] * keep) * tokens_rows).astype(bf16)
    norm_two_t = norm_two.T

    acc_s[...] = jnp.zeros_like(acc_s)
    for start, width in CHUNKS:

        @pl.when(hidden_count > start)
        def _(start=start, width=width):
            span = slice(start, start + width)
            mean_val, var_val = batch_stats(totals_ref[0, :, span], tokens_all)
            inv_bn = lax.rsqrt(var_val + norm_eps)
            front = inv_bn * gain_ref[:, span]
            shift_part = totals2_ref[0, 0:1, span] * (1.0 / tokens_all)
            gain_part = totals2_ref[0, 1:2, span] * (1.0 / tokens_all)
            lows = []
            for half in range(width // 128):
                low = start + half * 128
                part = slice(half * 128, half * 128 + 128)
                lane = slice(low, low + 128)
                pieces = []
                tap_totals = [jnp.zeros((1, 128), f32) for _ in range(9)]
                for i in range(images):
                    mine = slice(i * LP, (i + 1) * LP)
                    centred = (conv_ref[0, mine, lane] - mean_val[:, part]) * inv_bn[:, part]
                    conv_grad = (
                        front[:, part] * tokens
                        * (ng_ref[0, mine, lane] - shift_part[:, part] - centred * gain_part[:, part])
                    )
                    base = EDGE + i * HALO + COLS
                    halo_s[half, base : base + LP, :] = conv_grad
                    hidden = hid_ref[0, mine, lane].astype(f32)
                    acc = jnp.zeros((LP, 128), f32)
                    for a in range(3):
                        for b in range(3):
                            k = 3 * a + b
                            first = base - (a - 1) * COLS - (b - 1)
                            moved = halo_s[half, first : first + LP, :]
                            acc = acc + taps_ref[k : k + 1, lane] * moved
                            tap_totals[k] = tap_totals[k] + rows_sum(moved * hidden)
                    pieces.append(acc.astype(bf16))
                for k in range(9):
                    tapsg_ref[k : k + 1, lane] += tap_totals[k]
                lows.append(jnp.concatenate(pieces, axis=0))
            hidden_low = lows[0] if len(lows) == 1 else jnp.concatenate(lows, axis=1)
            fc1g_ref[:, span] += dot_nn(norm_two_t, hidden_low)
            acc_s[...] += dot_nt(hidden_low, fc1_ref[:, span])

    back = acc_s[...] * tokens_rows
    small_ref[0:1, :] += rows_sum(back * scaled_two)
    small_ref[1:2, :] += rows_sum(back) * keep
    residual_grad = og_ref[:, 0].reshape(rows, D).astype(f32) + norm_backward(
        back, scaled_two, inv_two, g2_ref[...], keep, inv_active
    )
    resg_ref[0] = residual_grad
    small_ref[2:3, :] += rows_sum((residual_grad * keep * tokens_rows).astype(bf16).astype(f32))


def attend_back_kernel(
    images, counts, actives, x_ref, resg_ref, e_ref, inv_ref, att_ref, kw_ref, g1_ref, b1_ref, wt_ref, w_ref,
    mix_ref, proj_ref, pick_qkv_ref, pick_proj_ref, pick_heads_ref,
    ing_ref, grads_ref, small_ref, talk_ref,
    projg_s, qkvg_s, qt_s, q_s, kt_s, v_s, mixc_s, da_s, dq_s, dk_s, dv_s,
):
    member = pl.program_id(0)
    heads = counts[member, 0]
    inv_active = actives[member, 0]
    rows = images * LP
    keep = kw_ref[0]
    tokens_rows = token_rows(rows)

    @pl.when(member == 0)
    def _():
        for ref in (projg_s, qkvg_s, small_ref, talk_ref):
            ref[...] = jnp.zeros_like(ref)

    x = x_ref[:, 0].reshape(rows, D).astype(f32)
    scaled_one, inv_one = norm_forward(x, keep, inv_active)
    norm_one = (scaled_one * g1_ref[...] + b1_ref[...] * keep).astype(bf16)
    residual_grad = resg_ref[0]
    proj_low = (residual_grad * keep * tokens_rows).astype(bf16)

    mix_t = mix_ref[0].T
    for h in range(H):
        mixc_s[h] = jnp.broadcast_to(mix_t[:, h : h + 1], (CP, 128))
    sum_lanes = lax.broadcasted_iota(jnp.int32, (1, VP), 1) % EP
    sum_lanes = ((sum_lanes == E) | (sum_lanes == E + 1)).astype(f32)
    active_rows = lax.broadcasted_iota(jnp.int32, (CP, 1), 0) < heads * E
    row_in_head = lax.broadcasted_iota(jnp.int32, (EP, 1), 0)
    for i in range(images):
        mine = slice(i * LP, (i + 1) * LP)
        n1 = norm_one[mine]
        queries = dot_nt(wt_ref[Q_ROWS, :], n1).astype(bf16).astype(f32)
        qt_s[i] = jnp.where(active_rows, queries, 0.0)
        q_s[i] = dot_nn(n1, w_ref[:, Q_ROWS]).astype(bf16)
        kt_s[i] = dot_nt(wt_ref[K_ROWS, :], n1).astype(bf16)
        v_s[i] = (dot_nn(n1, w_ref[:, V_ROWS]) + sum_lanes).astype(bf16)
        da_s[i] = dot_nt(proj_ref[...], proj_low[mine]).astype(bf16).astype(f32)
        projg_s[...] += dot_nn(att_ref[0, i].astype(bf16), proj_low[mine])
    dq_s[...] = jnp.zeros_like(dq_s)
    dk_s[...] = jnp.zeros_like(dk_s)
    dv_s[...] = jnp.zeros_like(dv_s)

    for pair in range(H // 2):

        @pl.when(heads > 2 * pair)
        def _(pair=pair):
            for h in (2 * pair, 2 * pair + 1):
                head = slice(h * EP, h * EP + EP)
                mix_row = mix_ref[0, h : h + 1, :]
                for i in range(images):
                    inv = inv_ref[0, i, h : h + 1, :]
                    up = da_s[i, head, :]
                    delta = rows_sum(jnp.where(row_in_head < E, up * att_ref[0, i, head, :], 0.0))
                    up = up * inv
                    delta = -delta * inv
                    delta_high = delta.astype(bf16).astype(f32)
                    up_low = jnp.where(
                        row_in_head == E, delta_high, jnp.where(row_in_head == E + 1, delta - delta_high, up)
                    ).astype(bf16)
                    e = e_ref[0, i, h]
                    diff = dot_nn(v_s[i, :, head], up_low)
                    grad = e * diff.astype(bf16)
                    dv_s[i, head, :] = dot_nt(up_low, e)
                    turned = dot_nn(kt_s[i], grad)
                    column = mixc_s[h]
                    column = jnp.concatenate([column, column[:, : LP - 128]], axis=1)
                    dq_s[i] += turned * column
                    moved = turned * qt_s[i]
                    talk_ref[h] += moved[:, 0:128] + jnp.pad(moved[:, 128:LP], ((0, 0), (0, 256 - LP)))
                    dk_s[i] += dot_nn(grad, q_s[i]) * mix_row

    parts = []
    for i in range(images):
        n1 = norm_one[i * LP : (i + 1) * LP]
        dq = dq_s[i].astype(bf16)
        dk = dk_s[i].astype(bf16).T
        dv = dv_s[i].astype(bf16)
        qkvg_s[Q_ROWS, :] += dot_nn(dq, n1)
        qkvg_s[K_ROWS, :] += dot_nn(dk, n1)
        qkvg_s[V_ROWS, :] += dot_nn(dv, n1)
        back_t = dot_nn(w_ref[:, Q_ROWS], dq) + dot_nn(w_ref[:, K_ROWS], dk) + dot_nn(w_ref[:, V_ROWS], dv)
        parts.append(back_t.T)
    back = jnp.concatenate(parts, axis=0) * tokens_rows
    small_ref[0:1, :] += rows_sum(back * scaled_one)
    small_ref[1:2, :] += rows_sum(back) * keep
    result = residual_grad + norm_backward(back, scaled_one, inv_one, g1_ref[...], keep, inv_active)
    ing_ref[:, 0] = result.reshape(images, LP, D)

    @pl.when(member == SUBNETS - 1)
    def _():
        qkv = dot_nn(pick_qkv_ref[...], qkvg_s[...].astype(bf16))
        proj = dot_nn(pick_heads_ref[...], projg_s[...].astype(bf16)).astype(bf16)
        grads_ref[...] = (qkv + dot_nt(pick_proj_ref[...], proj)).astype(bf16)


def whole(shape):
    return pl.BlockSpec(shape, lambda s: (0,) * len(shape))


def per_member(shape):
    return pl.BlockSpec((1,) + shape, lambda s: (s,) + (0,) * len(shape))


def per_image(images):
    return pl.BlockSpec((images, 1, LP, D), lambda s: (0, s, 0, 0))


SMEM = pl.BlockSpec(memory_space=pltpu.SMEM)


def sds(shape, dtype=f32):
    return jax.ShapeDtypeStruct(shape, dtype)


def params():
    return pltpu.CompilerParams(vmem_limit_bytes=56 * MIB, dimension_semantics=("arbitrary",))


def swap(value, axis, step=1):
    size = lax.axis_size(axis)
    return lax.ppermute(value, axis, [(i, i ^ step) for i in range(size)])


def steps_of(axis):
    step, size = 1, lax.axis_size(axis)
    while step < size:
        yield step
        step *= 2


def sum_over(value, axes):
    for axis in axes:
        for step in steps_of(axis):
            value = value + swap(value, axis, step)
    return value


def split_pair(value):
    high = value.astype(bf16)
    return high, (value - high.astype(f32)).astype(bf16)


def halves(value, dim, mine):
    low, high = jnp.split(value, 2, axis=dim)
    return jnp.where(mine == 0, low, high), jnp.where(mine == 0, high, low)


def sum_packed(big, small, axes):
    rows, extra = big.shape[0], small.shape[0]
    for axis in axes:
        for step in steps_of(axis):
            got = swap(jnp.concatenate((big,) + split_pair(small), axis=0), axis, step)
            big = (big.astype(f32) + got[:rows].astype(f32)).astype(bf16)
            small = small + (got[rows : rows + extra].astype(f32) + got[rows + extra :].astype(f32))
    return big, small


def in_order(mine, first, second, dim):
    return jnp.where(mine == 0, jnp.concatenate([first, second], dim), jnp.concatenate([second, first], dim))


def to_tokens(flat):
    images = flat.shape[0]
    grid = flat.reshape(images, SUBNETS, GRID, GRID, D)
    grid = jnp.pad(grid, ((0, 0), (0, 0), (0, 0), (0, COLS - GRID), (0, 0)))
    return grid.reshape(images, SUBNETS, LP, D)


def from_tokens(tokens):
    images = tokens.shape[0]
    grid = tokens.reshape(images, SUBNETS, GRID, COLS, D)[:, :, :, :GRID]
    return grid.reshape(images, SUBNETS * L * D)


def pad_to(value, axis, size):
    widths = [(0, 0)] * value.ndim
    widths[axis] = (0, size - value.shape[axis])
    return jnp.pad(value, widths)


def one_hot(rows, cols, pairs):
    out = np.zeros((rows, cols), np.float32)
    for r, c in pairs:
        out[r, c] = 1.0
    return out


def padded_column(j):
    part, rest = divmod(j, D)
    return part * 256 + (rest if part < 2 else rest // E * EP + rest % E)


HALF = D // 2
QKV_HALF = 3 * D // 2
PAIR = QKV_HALF + HALF
SPREAD = np.stack(
    [one_hot(QKV_HALF, WP, [(j, padded_column(c * QKV_HALF + j)) for j in range(QKV_HALF)]) for c in range(2)]
)
PLACE = np.stack([one_hot(D, HALF, [(c * HALF + j, j) for j in range(HALF)]) for c in range(2)])
HEADS = np.stack(
    [one_hot(VP, HALF, [((c * HALF + j) // E * EP + (c * HALF + j) % E, j) for j in range(HALF)]) for c in range(2)]
)
PICK_QKV = one_hot(
    2 * PAIR, WP, [(c * PAIR + j, padded_column(c * QKV_HALF + j)) for c in range(2) for j in range(QKV_HALF)]
)
PICK_PROJ = one_hot(2 * PAIR, D, [(c * PAIR + QKV_HALF + j, c * HALF + j) for c in range(2) for j in range(HALF)])
PICK_HEADS = one_hot(D, VP, [(j, j // E * EP + j % E) for j in range(D)])


def weight_kernel(place, a_ref, b_ref, c_ref, d_ref, spread_ref, place_ref, heads_ref, w_ref, wt_ref, proj_ref):
    row, col = place[0], place[1]
    weight = jnp.zeros((D, WP), f32)
    turned = jnp.zeros((WP, D), f32)
    proj = jnp.zeros((VP, D), f32)
    for ref, r, c in ((a_ref, row, col), (b_ref, 1 - row, col), (c_ref, row, 1 - col), (d_ref, 1 - row, 1 - col)):
        qkv = ref[:, :QKV_HALF]
        part = ref[:, QKV_HALF:]
        weight = weight + dot_nn(place_ref[r], dot_nn(qkv, spread_ref[c]).astype(bf16))
        wide = lax.dot_general(spread_ref[c], qkv, (((0,), (1,)), ((), ())), preferred_element_type=f32)
        turned = turned + dot_nt(wide.astype(bf16), place_ref[r])
        proj = proj + dot_nn(heads_ref[r], dot_nt(part, place_ref[c]).astype(bf16))
    w_ref[...] = weight.astype(bf16)
    wt_ref[...] = turned.astype(bf16)
    proj_ref[...] = proj.astype(bf16)


def body(
    block_in, out_grad, width_mask, head_mask, hidden_mask, qkv_weight, proj_weight, fc1_weight, fc2_weight,
    norm1_gain, norm1_shift, proj_bias, norm2_gain, second_norm_bias, conv_taps, bn_gain, bn_shift, output_bias,
    talk_mix,
):
    images = block_in.shape[0]
    rows = images * LP
    devices_all = lax.axis_size("dp") * lax.axis_size("row") * lax.axis_size("col")
    tokens_all = float(devices_all * images * L)
    row, col = lax.axis_index("row"), lax.axis_index("col")

    attend_own = jnp.concatenate([qkv_weight, proj_weight], axis=1)
    attend_row = swap(attend_own, "row")
    attend_col, attend_both = swap(attend_own, "col"), swap(attend_row, "col")
    hidden_own = jnp.stack([fc1_weight, fc2_weight.T])
    hidden_row = swap(hidden_own, "row")
    hidden_col, hidden_both = swap(hidden_own, "col"), swap(hidden_row, "col")

    w, wt, proj = pl.pallas_call(
        weight_kernel,
        in_specs=[SMEM] + [pl.BlockSpec(memory_space=pltpu.VMEM)] * 7,
        out_specs=[pl.BlockSpec(memory_space=pltpu.VMEM)] * 3,
        out_shape=[sds((D, WP), bf16), sds((WP, D), bf16), sds((VP, D), bf16)],
        name="weights",
    )(
        jnp.stack([row, col]), attend_own, attend_row, attend_col, attend_both,
        *(jnp.asarray(v, bf16) for v in (SPREAD, PLACE, HEADS)),
    )
    fc1 = in_order(
        col, in_order(row, hidden_own[0], hidden_row[0], 0), in_order(row, hidden_col[0], hidden_both[0], 0), 1
    )
    fc2 = in_order(
        row, in_order(col, hidden_own[1], hidden_col[1], 0), in_order(col, hidden_row[1], hidden_both[1], 0), 1
    ).T
    fc1 = pad_to(fc1, 1, FP)
    fc2 = pad_to(fc2, 0, FP)

    keep_w = width_mask.astype(f32)[:, None, :]
    keep_e = pad_to(hidden_mask.astype(bf16), 1, FP)[:, None, :]
    keep_h = head_mask.astype(f32)
    counts = jnp.stack([jnp.sum(head_mask, axis=1), jnp.sum(hidden_mask, axis=1)], axis=1)
    actives = 1.0 / jnp.sum(width_mask, axis=1, keepdims=True).astype(f32)
    mix = jnp.repeat(talk_mix[None] * keep_h[:, None, :] * HEAD_SCALE, E, axis=2)
    mix_back = pad_to(mix, 2, CP)
    mix_front = jnp.concatenate([mix * LOG2E, jnp.ones((SUBNETS, H, 1), f32)], axis=2)
    mix_front = pad_to(mix_front, 2, CP)
    g1, b1, pb, g2, b2, ob = (
        v[None] for v in (norm1_gain, norm1_shift, proj_bias, norm2_gain, second_norm_bias, output_bias)
    )
    taps = pad_to(conv_taps, 1, FP)
    gain, shift = (pad_to(v[None], 1, FP) for v in (bn_gain, bn_shift))

    x = to_tokens(block_in)
    og = to_tokens(out_grad)

    row_spec = per_member((rows, D))
    wide_spec = per_member((rows, FP))
    e_spec = per_member((images, H, LP, LP))
    inv_spec = per_member((images, H, LP))
    att_spec = per_member((images, VP, LP))
    sums_spec = per_member((2, FP))
    width_spec, one_wide, mix_spec = per_member((1, D)), per_member((1, FP)), per_member((H, CP))
    vec, wide_vec, taps_spec = whole((1, D)), whole((1, FP)), whole((9, FP))
    w_spec, wt_spec, proj_spec = whole((D, WP)), whole((WP, D)), whole((VP, D))
    halo = pltpu.VMEM((2, EDGE + images * HALO + EDGE, 128), f32)

    e, inv, att, res = pl.pallas_call(
        functools.partial(attend_kernel, images),
        grid=(SUBNETS,),
        in_specs=[
            SMEM, SMEM, per_image(images), width_spec, vec, vec, wt_spec, w_spec, mix_spec, proj_spec, vec,
        ],
        out_specs=[e_spec, inv_spec, att_spec, row_spec],
        out_shape=[
            sds((SUBNETS, images, H, LP, LP), bf16), sds((SUBNETS, images, H, LP)), sds((SUBNETS, images, VP, LP)),
            sds((SUBNETS, rows, D)),
        ],
        scratch_shapes=[
            pltpu.VMEM((images, CP, LP), bf16), pltpu.VMEM((images, LP, CP), f32), pltpu.VMEM((images, VP, LP), bf16),
        ],
        compiler_params=params(),
        name="attend",
    )(counts, actives, x, keep_w, g1, b1, wt, w, mix_front, proj, pb)

    hid, conv, sums = pl.pallas_call(
        functools.partial(hidden_kernel, images),
        grid=(SUBNETS,),
        in_specs=[SMEM, SMEM, row_spec, width_spec, one_wide, vec, vec, whole((D, FP)), taps_spec],
        out_specs=[wide_spec, wide_spec, sums_spec],
        out_shape=[sds((SUBNETS, rows, FP), bf16), sds((SUBNETS, rows, FP)), sds((SUBNETS, 2, FP))],
        scratch_shapes=[halo],
        compiler_params=params(),
        name="hidden",
    )(counts, actives, res, keep_w, keep_e, g2, b2, fc1, taps)

    totals = sum_over(sums, ("col", "row", "dp"))

    block_out, ng, sums2, fc2_grad_t, out_bias_grad, bn_mean, bn_var = pl.pallas_call(
        functools.partial(middle_kernel, images, tokens_all),
        grid=(SUBNETS,),
        in_specs=[
            SMEM, wide_spec, row_spec, per_image(images), width_spec, one_wide, whole((FP, D)), vec,
            wide_vec, wide_vec, sums_spec,
        ],
        out_specs=[per_image(images), wide_spec, sums_spec, whole((D, FP)), vec, one_wide, one_wide],
        out_shape=[
            sds((images, SUBNETS, LP, D)), sds((SUBNETS, rows, FP)), sds((SUBNETS, 2, FP)), sds((D, FP)),
            sds((1, D)), sds((SUBNETS, 1, FP)), sds((SUBNETS, 1, FP)),
        ],
        scratch_shapes=[pltpu.VMEM((rows, D), f32)],
        compiler_params=params(),
        name="middle",
    )(counts, conv, res, og, keep_w, keep_e, fc2, ob, gain, shift, totals)

    totals2 = sum_over(sums2, ("col", "row", "dp"))

    res_grad, fc1_grad, taps_grad, small1 = pl.pallas_call(
        functools.partial(hidden_back_kernel, images, tokens_all),
        grid=(SUBNETS,),
        in_specs=[
            SMEM, SMEM, per_image(images), row_spec, wide_spec, wide_spec, wide_spec, width_spec, vec, vec,
            whole((D, FP)), taps_spec, wide_vec, sums_spec, sums_spec,
        ],
        out_specs=[row_spec, whole((D, FP)), taps_spec, whole((8, D))],
        out_shape=[sds((SUBNETS, rows, D)), sds((D, FP)), sds((9, FP)), sds((8, D))],
        scratch_shapes=[halo, pltpu.VMEM((rows, D), f32)],
        compiler_params=params(),
        name="hidden_back",
    )(counts, actives, og, res, hid, conv, ng, keep_w, g2, b2, fc1, taps, gain, totals, totals2)

    fc1_keep, fc1_send = halves(fc1_grad[:, :FF].astype(bf16), 1, col)
    fc2_keep, fc2_send = halves(fc2_grad_t[:, :FF].astype(bf16), 0, col)
    flat = jnp.concatenate([taps_grad[:, :FF].reshape(-1), small1[:3].reshape(-1), out_bias_grad.reshape(-1)])
    small_rows = pl.cdiv(flat.shape[0], 8 * FF // 2) * 8
    flat = pad_to(flat, 0, small_rows * FF // 2).reshape(small_rows, FF // 2)
    flat = flat + swap(flat, "col")
    fc1_keep, fc1_send = halves(fc1_keep + swap(fc1_send, "col"), 0, row)
    fc2_keep, fc2_send = halves(fc2_keep + swap(fc2_send, "col"), 1, row)
    got = swap(jnp.concatenate([fc1_send, fc2_send], axis=0), "row")
    flat = flat + swap(flat, "row")
    hidden_grads, flat = sum_packed(jnp.concatenate([fc1_keep, fc2_keep], axis=0) + got, flat, ("dp",))
    flat = flat.reshape(-1)
    taps_grad = flat[: 9 * FF].reshape(9, FF)
    n2g, n2s, pbg, obg = (flat[9 * FF + i * D : 9 * FF + (i + 1) * D] for i in range(4))

    in_grad, grads, small2, talk = pl.pallas_call(
        functools.partial(attend_back_kernel, images),
        grid=(SUBNETS,),
        in_specs=[
            SMEM, SMEM, per_image(images), row_spec, e_spec, inv_spec, att_spec, width_spec, vec, vec, wt_spec, w_spec,
            mix_spec, proj_spec, whole((2 * PAIR, WP)), whole((2 * PAIR, D)), whole((D, VP)),
        ],
        out_specs=[per_image(images), whole((2 * PAIR, D)), whole((8, D)), whole((H, CP, 128))],
        out_shape=[sds((images, SUBNETS, LP, D)), sds((2 * PAIR, D), bf16), sds((8, D)), sds((H, CP, 128))],
        scratch_shapes=[
            pltpu.VMEM((VP, D), f32),
            pltpu.VMEM((WP, D), f32),
            pltpu.VMEM((images, CP, LP), f32),
            pltpu.VMEM((images, LP, CP), bf16),
            pltpu.VMEM((images, CP, LP), bf16),
            pltpu.VMEM((images, LP, VP), bf16),
            pltpu.VMEM((H, CP, 128), f32),
            pltpu.VMEM((images, VP, LP), f32),
            pltpu.VMEM((images, CP, LP), f32),
            pltpu.VMEM((images, LP, CP), f32),
            pltpu.VMEM((images, VP, LP), f32),
        ],
        compiler_params=params(),
        name="attend_back",
    )(
        counts, actives, x, res_grad, e, inv, att, keep_w, g1, b1, wt, w, mix_back, proj,
        *(jnp.asarray(v, bf16) for v in (PICK_QKV, PICK_PROJ, PICK_HEADS)),
    )

    talk_grad = jnp.sum(talk[:, :D].reshape(H, H, E * 128), axis=2) * HEAD_SCALE
    tail = jnp.concatenate([small2[:2].reshape(-1), talk_grad.reshape(-1)])
    tail = pad_to(tail, 0, 16 * HALF).reshape(16, HALF)
    keep, send = halves(grads, 0, col)
    tail = tail + swap(tail, "col")
    keep, send = halves(keep + swap(send, "col"), 1, row)
    tail = tail + swap(tail, "row")
    attend_grads, tail = sum_packed(keep + swap(send, "row"), tail, ("dp",))
    tail = tail.reshape(-1)
    n1g, n1s, talk_grad = tail[:D], tail[D : 2 * D], tail[2 * D : 2 * D + H * H].reshape(H, H)

    bn_grads = jnp.sum(totals2, axis=0)[:, :FF]
    return (
        from_tokens(block_out), from_tokens(in_grad),
        attend_grads[:QKV_HALF].T.astype(f32), attend_grads[QKV_HALF:].T.astype(f32),
        hidden_grads[:HALF].astype(f32), hidden_grads[HALF:].T.astype(f32),
        n1g, n1s, pbg, n2g, n2s, taps_grad, bn_grads[1], bn_grads[0], obg, talk_grad,
        bn_mean[:, 0, :FF], bn_var[:, 0, :FF],
    )


def solution(mesh):
    split = P(AXES, None)
    weight = P("row", "col")
    in_specs = (split, split, P(), P(), P()) + (weight,) * 4 + (P(),) * 10
    out_specs = (split, split) + (weight,) * 4 + (P(),) * 12
    return jax.shard_map(body, mesh=mesh, in_specs=in_specs, out_specs=out_specs, check_vma=False)
```

```python
import functools
import math

import jax
import jax.numpy as jnp
import numpy as np
from jax import lax
from jax.experimental import pallas as pl
from jax.experimental.pallas import tpu as pltpu
from jax.sharding import PartitionSpec as P

H = 12
E = 18
GRID = 14
SUBNETS = 4
D = 216
FF = 864
L = 196

COLS = 16
LP = GRID * COLS
CP = 224
EP = 32
VP = H * EP
CHUNK = 256
CHUNKS = tuple((start, min(CHUNK, FF - start)) for start in range(0, FF, CHUNK))
CHUNK_COUNTS = (2, 3, 4)
HEAD_COUNTS = (8, 10, 12)
HALO = COLS + LP + COLS
EDGE = 8
BLOCK = LP // 2
MIB = 1 << 20
Q_ROWS, K_ROWS, V_ROWS = slice(0, CP), slice(256, 256 + CP), slice(512, 512 + VP)
WP = 896
HALF = D // 2
QKV_HALF = 3 * D // 2
SMALL = (9 * FF + 4 * D) // HALF
PAIR = QKV_HALF + HALF
LAG = 3
SLOTS = 2 * LAG + 1

norm_eps = 1e-05
f32 = jnp.float32
bf16 = jnp.bfloat16
AXES = ("dp", "row", "col")
HEAD_SCALE = 1.0 / math.sqrt(E)
LOG2E = math.log2(math.e)


def dot_nn(a, b):
    return lax.dot_general(a, b, (((1,), (0,)), ((), ())), preferred_element_type=f32)


def dot_nt(a, b):
    return lax.dot_general(a, b, (((1,), (1,)), ((), ())), preferred_element_type=f32)


def token_mask(rows):
    return (lax.broadcasted_iota(jnp.int32, (rows, 1), 0) % COLS < GRID).astype(f32)


def masked(value, mask):
    rows, lanes = value.shape
    return (value.reshape(rows // COLS, COLS, lanes) * mask).reshape(rows, lanes)


def norm_forward(values, keep, inv_active):
    mean_val = jnp.sum(values * keep, axis=-1, keepdims=True) * inv_active
    centred = (values - mean_val) * keep
    var_val = jnp.sum(centred * centred, axis=-1, keepdims=True) * inv_active
    inv_std = lax.rsqrt(var_val + norm_eps)
    return centred * inv_std, inv_std


def norm_backward(upstream, scaled, inv_std, gain, keep, inv_active):
    scaled_grad = upstream * gain
    first = jnp.sum(scaled_grad * keep, axis=-1, keepdims=True) * inv_active
    second = jnp.sum(scaled_grad * scaled, axis=-1, keepdims=True) * inv_active
    return keep * inv_std * (scaled_grad - first - scaled * second)


def rows_sum(v):
    return jnp.sum(v, axis=0, keepdims=True)


def fold_rows(v):
    parts = [v[r : r + 8] for r in range(0, v.shape[0], 8)]
    while len(parts) > 1:
        parts = [sum(parts[j : j + 2]) for j in range(0, len(parts), 2)]
    return parts[0]


def blocks(rows, size=BLOCK):
    return [slice(start, start + size) for start in range(0, rows, size)]


def lane_parts(start, width):
    return [slice(low, min(low + 128, start + width)) for low in range(start, start + width, 128)]


def width_of(width_ref, member):
    keep = width_ref[pl.ds(member, 1), :].astype(f32)
    return keep, 1.0 / jnp.sum(keep, axis=1, keepdims=True)


def has_heads(heads, member, count):
    right = heads[member, count - 1] > 0
    return right & (heads[member, count] == 0) if count < H else right


def has_chunks(hiddens, member, count):
    right = hiddens[member, CHUNKS[count - 1][0]] > 0
    return right & (hiddens[member, CHUNKS[count][0]] == 0) if count < len(CHUNKS) else right


def head_lanes():
    row = lax.broadcasted_iota(jnp.int32, (H, CP), 0) * E
    lane = lax.broadcasted_iota(jnp.int32, (H, CP), 1)
    return ((lane >= row) & (lane < row + E)).astype(f32)


def mix_rows(talk_ref, head_ref, member, factor):
    scaled = talk_ref[...] * (head_ref[pl.ds(member, 1), :].astype(f32) * factor)
    return lax.dot_general(
        scaled, head_lanes(), (((1,), (0,)), ((), ())), precision=lax.Precision.HIGHEST, preferred_element_type=f32
    )


def attend_kernel(
    images, heads, x_ref, width_ref, head_ref, talk_ref, g1_ref, b1_ref, wt_ref, w_ref, proj_ref, pb_ref,
    e_ref, inv_ref, att_ref, res_ref, n1_s, qt_s, k_s, vt_s, s_s, mix_s,
):
    member = pl.program_id(0)
    rows = images * LP
    keep, inv_active = width_of(width_ref, member)
    for i in range(images):
        for block in blocks(LP):
            scaled, _ = norm_forward(x_ref[i, 0, block, :].astype(f32), keep, inv_active)
            n1_s[i, block, :] = (scaled * g1_ref[...] + b1_ref[...] * keep).astype(bf16)

    ones_row = (lax.broadcasted_iota(jnp.int32, (CP, 1), 0) == D).astype(f32)
    mask_lane = (lax.broadcasted_iota(jnp.int32, (1, CP), 1) == D).astype(f32)
    sum_rows = (lax.broadcasted_iota(jnp.int32, (VP, 1), 0) % EP == E).astype(f32)
    key_mask = (1.0 - token_mask(LP)) * (-1e30) * mask_lane
    mix_s[...] = mix_rows(talk_ref, head_ref, member, HEAD_SCALE * LOG2E) + mask_lane
    for i in range(images):
        mine = n1_s[i]
        qt_s[i] = (dot_nt(wt_ref[Q_ROWS, :], mine) + ones_row).astype(bf16)
        k_s[i] = dot_nn(mine, w_ref[:, K_ROWS]).astype(bf16).astype(f32) + key_mask
        vt_s[i] = (dot_nt(wt_ref[V_ROWS, :], mine) + sum_rows).astype(bf16)
    att_ref[...] = jnp.zeros_like(att_ref)

    def scores(h, i, slot):
        keys = (k_s[i] * mix_s[h : h + 1, :]).astype(bf16)
        s_s[slot] = dot_nn(keys, qt_s[i])

    def soften(h, i, slot):
        for part in lane_parts(0, LP):
            mixed = s_s[slot, :, part]
            peak = jnp.max(mixed, axis=0, keepdims=True)
            e_ref[0, i, h, :, part] = jnp.exp2(mixed - peak).astype(bf16)

    def attend(h, i):
        head = slice(h * EP, h * EP + EP)
        out = dot_nn(vt_s[i, head, :], e_ref[0, i, h])
        inv = 1.0 / out[E : E + 1]
        inv_ref[0, i, h : h + 1, :] = inv
        att_ref[0, i, head, :] = (out * inv).astype(bf16)

    for count in HEAD_COUNTS:

        @pl.when(has_heads(heads, member, count))
        def _(count=count):
            units = [(h, i) for h in range(count) for i in range(images)]
            for t in range(len(units) + 2 * LAG):
                if t < len(units):
                    scores(*units[t], t % SLOTS)
                if LAG <= t < len(units) + LAG:
                    soften(*units[t - LAG], (t - LAG) % SLOTS)
                if t >= 2 * LAG:
                    attend(*units[t - 2 * LAG])

    for i in range(images):
        attended = att_ref[0, i].T
        out = dot_nn(attended, proj_ref[...]) + pb_ref[...]
        res_ref[0, i * LP : (i + 1) * LP, :] = x_ref[i, 0].astype(f32) + keep * out


def hidden_kernel(
    images, hiddens, res_ref, width_ref, hidden_ref, g2_ref, b2_ref, fc1_ref, taps_ref,
    hid_ref, conv_ref, sums_ref, n2_s, halo_s,
):
    member = pl.program_id(0)
    rows = images * LP
    keep, inv_active = width_of(width_ref, member)
    tokens = token_mask(COLS)
    for block in blocks(rows):
        scaled, _ = norm_forward(res_ref[0, block, :], keep, inv_active)
        n2_s[block, :] = masked(scaled * g2_ref[...] + b2_ref[...] * keep, tokens).astype(bf16)
    sums_ref[member] = jnp.zeros(sums_ref.shape[1:], f32)
    keep_e = hidden_ref[pl.ds(member, 1), :].astype(f32)

    @pl.when(member == 0)
    def _():
        halo_s[...] = jnp.zeros_like(halo_s)

    def project(start, width, slot):
        span = slice(start, start + width)
        hidden = dot_nt(n2_s[...], fc1_ref[span, :])
        hid_ref[0, :, span] = hidden.astype(bf16)
        for half, lane in enumerate(lane_parts(start, width)):
            size = lane.stop - lane.start
            for i in range(images):
                base = EDGE + i * HALO + COLS
                halo_s[slot, half, base : base + LP, :size] = hidden[
                    i * LP : (i + 1) * LP, lane.start - start : lane.stop - start
                ]

    def convolve(start, width, slot):
        for half, lane in enumerate(lane_parts(start, width)):
            size = lane.stop - lane.start
            taps = taps_ref[:, lane] * keep_e[:, lane]
            total = jnp.zeros((8, size), f32)
            total_square = jnp.zeros((8, size), f32)
            for i in range(images):
                base = EDGE + i * HALO + COLS
                for block in blocks(LP):
                    acc = jnp.zeros((BLOCK, size), f32)
                    for a in range(3):
                        for b in range(3):
                            first = base + block.start + (a - 1) * COLS + b - 1
                            tap = taps[3 * a + b : 3 * a + b + 1, :]
                            acc = acc + tap * halo_s[slot, half, first : first + BLOCK, :size]
                    conv_ref[0, i * LP + block.start : i * LP + block.stop, lane] = acc
                    valid = masked(acc, tokens)
                    total = total + fold_rows(valid)
                    total_square = total_square + fold_rows(valid * acc)
            sums_ref[member, 0:1, lane] = rows_sum(total)
            sums_ref[member, 1:2, lane] = rows_sum(total_square)

    for count in CHUNK_COUNTS:

        @pl.when(has_chunks(hiddens, member, count))
        def _(count=count):
            for n in range(count + 1):
                if n < count:
                    project(*CHUNKS[n], n % 2)
                if n > 0:
                    convolve(*CHUNKS[n - 1], (n - 1) % 2)


def front_kernel(
    images, heads, hiddens, x_ref, width_ref, head_ref, hidden_ref, talk_ref, g1_ref, b1_ref, wt_ref, w_ref, proj_ref,
    pb_ref, g2_ref, b2_ref, fc1_ref, taps_ref, e_ref, inv_ref, att_ref, res_ref, hid_ref, conv_ref, sums_ref,
    n1_s, qt_s, k_s, vt_s, s_s, mix_s, n2_s, halo_s,
):
    attend_kernel(
        images, heads, x_ref, width_ref, head_ref, talk_ref, g1_ref, b1_ref, wt_ref, w_ref, proj_ref, pb_ref,
        e_ref, inv_ref, att_ref, res_ref, n1_s, qt_s, k_s, vt_s, s_s, mix_s,
    )
    hidden_kernel(
        images, hiddens, res_ref, width_ref, hidden_ref, g2_ref, b2_ref, fc1_ref, taps_ref,
        hid_ref, conv_ref, sums_ref, n2_s, halo_s,
    )


def batch_stats(totals, tokens_all):
    mean_val = totals[0:1] * (1.0 / tokens_all)
    var_val = totals[1:2] * (1.0 / tokens_all) - mean_val * mean_val
    return mean_val, var_val


def middle_kernel(
    images, tokens_all, hiddens, place, conv_ref, res_ref, og_ref, width_ref, hidden_ref, fc2_ref, ob_ref, gain_ref,
    shift_ref, totals_ref, out_ref, ng_ref, sums_ref, mine_ref, send_ref, obg_ref, mean_ref, var_ref,
    low_s, acc_s, swish_s, up_s, fc2g_s,
):
    member = pl.program_id(0)
    rows = images * LP
    keep, _ = width_of(width_ref, member)

    @pl.when(member == 0)
    def _():
        fc2g_s[...] = jnp.zeros_like(fc2g_s)
        obg_ref[...] = jnp.zeros_like(obg_ref)

    bias_total = jnp.zeros((8, D), f32)
    for i in range(images):
        for block in blocks(LP):
            out_low = (og_ref[i, 0, block, :].astype(f32) * keep).astype(bf16)
            low_s[i * LP + block.start : i * LP + block.stop, :] = out_low
            bias_total = bias_total + fold_rows(out_low.astype(f32))
    obg_ref[...] += rows_sum(bias_total)
    out_low_t = low_s[...].T
    sums_ref[member] = jnp.zeros(sums_ref.shape[1:], f32)
    keep_e = hidden_ref[pl.ds(member, 1), :].astype(f32)
    mean_all, var_all = batch_stats(totals_ref[member], tokens_all)
    mean_ref[pl.ds(member, 1), :] = mean_all
    var_ref[pl.ds(member, 1), :] = var_all
    acc_s[...] = jnp.zeros_like(acc_s)

    def pull(start, width, slot):
        up_s[slot, :, :width] = dot_nt(low_s[...], fc2_ref[start : start + width, :])

    def gates(start, width, slot):
        for lane in lane_parts(start, width):
            inner = slice(lane.start - start, lane.stop - start)
            size = lane.stop - lane.start
            mean_val, var_val = batch_stats(totals_ref[member, :, lane], tokens_all)
            inv_bn = lax.rsqrt(var_val + norm_eps)
            kept = keep_e[:, lane]
            gain, shift = gain_ref[:, lane], shift_ref[:, lane]
            total = jnp.zeros((8, size), f32)
            total_gain = jnp.zeros((8, size), f32)
            for block in blocks(rows):
                centred = (conv_ref[0, block, lane] - mean_val) * inv_bn
                normed = centred * gain + shift
                gate = 0.5 * jnp.tanh(0.5 * normed) + 0.5
                kept_gate = gate * kept
                swish_s[slot, block, inner] = (normed * kept_gate).astype(bf16)
                normed_grad = up_s[slot, block, inner] * (kept_gate * (1.0 + normed * (1.0 - gate)))
                ng_ref[0, block, lane] = normed_grad.astype(bf16)
                total = total + fold_rows(normed_grad)
                total_gain = total_gain + fold_rows(normed_grad * centred)
            sums_ref[member, 0:1, lane] = rows_sum(total)
            sums_ref[member, 1:2, lane] = rows_sum(total_gain)

    def push(start, width, slot):
        span = slice(start, start + width)
        acc_s[...] += dot_nn(swish_s[slot, :, :width], fc2_ref[span, :])
        fc2g_s[:, span] += dot_nn(out_low_t, swish_s[slot, :, :width])

    for count in CHUNK_COUNTS:

        @pl.when(has_chunks(hiddens, member, count))
        def _(count=count):
            for n in range(count + 2):
                if n < count:
                    pull(*CHUNKS[n], n % 2)
                if 0 < n <= count:
                    gates(*CHUNKS[n - 1], (n - 1) % 2)
                if n > 1:
                    push(*CHUNKS[n - 2], (n - 2) % 2)

    for i in range(images):
        mine = slice(i * LP, (i + 1) * LP)
        out_ref[i, 0] = res_ref[0, mine, :] + keep * (acc_s[mine, :] + ob_ref[...])

    @pl.when(member == SUBNETS - 1)
    def _():
        low, high = fc2g_s[:HALF, :].T.astype(bf16), fc2g_s[HALF:, :].T.astype(bf16)
        mine_ref[...] = jnp.where(place[1] == 0, low, high)
        send_ref[...] = jnp.where(place[1] == 0, high, low)


def hidden_back_kernel(
    images, tokens_all, hiddens, place, obg_ref, og_ref, res_ref, hid_ref, conv_ref, ng_ref, width_ref, g2_ref, b2_ref,
    fc1_ref, taps_ref, gain_ref, totals_ref, totals2_ref,
    resg_ref, mine_ref, send_ref, small_ref, halo_s, acc_s, n2_s, low_s, fc1g_s, halves_s, tapsg_s, norm_s,
    scaled_s, inv_s,
):
    member = pl.program_id(0)
    rows = images * LP
    keep, inv_active = width_of(width_ref, member)
    tokens = token_mask(COLS)

    @pl.when(member == 0)
    def _():
        halo_s[...] = jnp.zeros_like(halo_s)
        for ref in (fc1g_s, tapsg_s, norm_s):
            ref[...] = jnp.zeros_like(ref)

    for block in blocks(rows):
        scaled, inv_std = norm_forward(res_ref[0, block, :], keep, inv_active)
        n2_s[block, :] = masked(scaled * g2_ref[...] + b2_ref[...] * keep, tokens).astype(bf16)
        scaled_s[block, :] = scaled
        inv_s[block, :] = inv_std
    norm_two_t = n2_s[...].T
    acc_s[...] = jnp.zeros_like(acc_s)

    def pull(start, width, slot):
        for half, lane in enumerate(lane_parts(start, width)):
            size = lane.stop - lane.start
            inner = slice(lane.start - start, lane.stop - start)
            mean_val, var_val = batch_stats(totals_ref[member, :, lane], tokens_all)
            inv_bn = lax.rsqrt(var_val + norm_eps)
            front = inv_bn * gain_ref[:, lane]
            shift_part = totals2_ref[member, 0:1, lane] * (1.0 / tokens_all)
            gain_part = totals2_ref[member, 1:2, lane] * (1.0 / tokens_all)
            for i in range(images):
                base = EDGE + i * HALO + COLS
                for block in blocks(LP):
                    mine = slice(i * LP + block.start, i * LP + block.stop)
                    centred = (conv_ref[0, mine, lane] - mean_val) * inv_bn
                    conv_grad = front * (ng_ref[0, mine, lane].astype(f32) - shift_part - centred * gain_part)
                    halo_s[slot, half, base + block.start : base + block.stop, :size] = masked(conv_grad, tokens)
            tap_totals = [jnp.zeros((8, size), f32) for _ in range(9)]
            for i in range(images):
                base = EDGE + i * HALO + COLS
                for block in blocks(LP):
                    mine = slice(i * LP + block.start, i * LP + block.stop)
                    hidden = hid_ref[0, mine, lane].astype(f32)
                    acc = jnp.zeros((BLOCK, size), f32)
                    for a in range(3):
                        for b in range(3):
                            k = 3 * a + b
                            first = base + block.start - (a - 1) * COLS - (b - 1)
                            moved = halo_s[slot, half, first : first + BLOCK, :size]
                            acc = acc + taps_ref[k : k + 1, lane] * moved
                            tap_totals[k] = tap_totals[k] + fold_rows(moved * hidden)
                    low_s[slot, mine, inner] = acc.astype(bf16)
            for k in range(9):
                tapsg_s[k : k + 1, lane] += rows_sum(tap_totals[k])

    def push(start, width, slot):
        span = slice(start, start + width)
        fc1g_s[:, span] += dot_nn(norm_two_t, low_s[slot, :, :width])
        acc_s[...] += dot_nn(low_s[slot, :, :width], fc1_ref[span, :])

    for count in CHUNK_COUNTS:

        @pl.when(has_chunks(hiddens, member, count))
        def _(count=count):
            for n in range(count + 1):
                if n < count:
                    pull(*CHUNKS[n], n % 2)
                if n > 0:
                    push(*CHUNKS[n - 1], (n - 1) % 2)

    gain_total = jnp.zeros((8, D), f32)
    shift_total = jnp.zeros((8, D), f32)
    bias_total = jnp.zeros((8, D), f32)
    for i in range(images):
        for block in blocks(LP):
            mine = slice(i * LP + block.start, i * LP + block.stop)
            scaled, inv_std = scaled_s[mine, :], inv_s[mine, :]
            back = masked(acc_s[mine, :], tokens)
            gain_total = gain_total + fold_rows(back * scaled)
            shift_total = shift_total + fold_rows(back)
            residual_grad = og_ref[i, 0, block, :].astype(f32) + norm_backward(
                back, scaled, inv_std, g2_ref[...], keep, inv_active
            )
            resg_ref[0, mine, :] = residual_grad
            proj_low = masked(residual_grad * keep, tokens).astype(bf16)
            bias_total = bias_total + fold_rows(proj_low.astype(f32))
    norm_s[0:1, :] += rows_sum(gain_total)
    norm_s[1:2, :] += rows_sum(shift_total) * keep
    norm_s[2:3, :] += rows_sum(bias_total)

    @pl.when(member == SUBNETS - 1)
    def _():
        halves_s[...] = fc1g_s[...].T.astype(bf16)
        mine_ref[...] = halves_s[pl.ds(pl.multiple_of(place[1] * (FF // 2), 16), FF // 2), :]
        send_ref[...] = halves_s[pl.ds(pl.multiple_of((1 - place[1]) * (FF // 2), 16), FF // 2), :]
        for k in range(FF // HALF):
            small_ref[pl.ds(k, 9, stride=FF // HALF), :] = tapsg_s[:, k * HALF : (k + 1) * HALF]
        norm_s[3:4, :] = obg_ref[...]
        for k in range(4):
            for part in range(2):
                row = 9 * FF // HALF + 2 * k + part
                small_ref[row : row + 1, :] = norm_s[k : k + 1, part * HALF : (part + 1) * HALF]


def attend_back_kernel(
    images, heads, place, x_ref, resg_ref, e_ref, inv_ref, att_ref, width_ref, head_ref, talkmix_ref, g1_ref, b1_ref,
    wt_ref, w_ref, proj_ref, pick_heads_ref,
    ing_ref, mine_ref, send_ref, small_ref, talk_s, norm_s, grads_s, projg_s, qkvg_s, n1_s, low_s, q_s, k_s, kt_s, v_s, mix_s, mixc_s, da_s, dq_s, dk_s, dv_s, up_s, diff_s, grad_s,
    back_s, scaled_s, inv_s,
):
    member = pl.program_id(0)
    keep, inv_active = width_of(width_ref, member)
    tokens = token_mask(COLS)

    @pl.when(member == 0)
    def _():
        for ref in (projg_s, qkvg_s, norm_s, talk_s):
            ref[...] = jnp.zeros_like(ref)

    for i in range(images):
        for block in blocks(LP):
            scaled, inv_std = norm_forward(x_ref[i, 0, block, :].astype(f32), keep, inv_active)
            n1_s[i, block, :] = (scaled * g1_ref[...] + b1_ref[...] * keep).astype(bf16)
            scaled_s[i, block, :] = scaled
            inv_s[i, block, :] = inv_std
            residual_grad = resg_ref[0, i * LP + block.start : i * LP + block.stop, :]
            low_s[i, block, :] = masked(residual_grad * keep, tokens).astype(bf16)

    mix = mix_rows(talkmix_ref, head_ref, member, HEAD_SCALE)
    mix_s[...] = mix
    mix_t = mix.T
    for h in range(H):
        mixc_s[h] = jnp.broadcast_to(mix_t[:, h : h + 1], (CP, 128))
    sum_lanes = lax.broadcasted_iota(jnp.int32, (1, VP), 1) % EP
    sum_lanes = ((sum_lanes == E) | (sum_lanes == E + 1)).astype(f32)
    row_in_head = lax.broadcasted_iota(jnp.int32, (EP, 1), 0)
    active = jnp.sum(head_ref[pl.ds(member, 1), :], axis=1, keepdims=True) * E
    active_lanes = lax.broadcasted_iota(jnp.int32, (1, CP), 1) < active
    for i in range(images):
        n1 = n1_s[i]
        q_s[i] = dot_nn(n1, w_ref[:, Q_ROWS]).astype(bf16)
        keys = dot_nn(n1, w_ref[:, K_ROWS]).astype(bf16).astype(f32)
        k_s[i] = jnp.where(active_lanes, keys, 0.0)
        kt_s[i] = dot_nt(wt_ref[K_ROWS, :], n1).astype(bf16)
        v_s[i] = (dot_nn(n1, w_ref[:, V_ROWS]) + sum_lanes).astype(bf16)
        da_s[i] = dot_nt(proj_ref[...], low_s[i]).astype(bf16).astype(f32)
        projg_s[...] += dot_nn(att_ref[0, i], low_s[i])
    dq_s[...] = jnp.zeros_like(dq_s)
    dk_s[...] = jnp.zeros_like(dk_s)
    dv_s[...] = jnp.zeros_like(dv_s)

    def stage_a(pair, i, slot):
        for k in range(2):
            h = 2 * pair + k
            head = slice(h * EP, h * EP + EP)
            inv = inv_ref[0, i, h : h + 1, :]
            up = da_s[i, head, :]
            delta = rows_sum(jnp.where(row_in_head < E, up * att_ref[0, i, head, :].astype(f32), 0.0))
            up = up * inv
            delta = -delta * inv
            delta_high = delta.astype(bf16).astype(f32)
            up_low = jnp.where(
                row_in_head == E, delta_high, jnp.where(row_in_head == E + 1, delta - delta_high, up)
            ).astype(bf16)
            up_s[slot, k] = up_low
            diff_s[slot, k] = dot_nn(v_s[i, :, head], up_low)

    def stage_b(pair, i, slot):
        for k in range(2):
            grad_s[slot, k] = e_ref[0, i, 2 * pair + k] * diff_s[slot, k].astype(bf16)

    def stage_c(pair, i, slot):
        for k in range(2):
            h = 2 * pair + k
            dv_s[i, h * EP : h * EP + EP, :] = dot_nt(up_s[slot, k], e_ref[0, i, h])
        query_part = 0.0
        key_part = 0.0
        for k in range(2):
            h = 2 * pair + k
            column = mixc_s[h]
            column = jnp.concatenate([column, column[:, : LP - 128]], axis=1)
            query_part = query_part + dot_nn(kt_s[i], grad_s[slot, k]) * column
            turned = dot_nn(grad_s[slot, k], q_s[i])
            key_part = key_part + turned * mix_s[h : h + 1, :]
            talk_s[h] += fold_rows(turned * k_s[i])
        dq_s[i] += query_part
        dk_s[i] += key_part

    for count in HEAD_COUNTS:

        @pl.when(has_heads(heads, member, count))
        def _(count=count):
            units = [(pair, i) for pair in range(count // 2) for i in range(images)]
            for t in range(len(units) + 2 * LAG):
                if t < len(units):
                    stage_a(*units[t], t % SLOTS)
                if LAG <= t < len(units) + LAG:
                    stage_b(*units[t - LAG], (t - LAG) % SLOTS)
                if t >= 2 * LAG:
                    stage_c(*units[t - 2 * LAG], (t - 2 * LAG) % SLOTS)

    for i in range(images):
        n1 = n1_s[i]
        dq = dq_s[i].astype(bf16)
        dk = dk_s[i].astype(bf16).T
        dv = dv_s[i].astype(bf16)
        qkvg_s[Q_ROWS, :] += dot_nn(dq, n1)
        qkvg_s[K_ROWS, :] += dot_nn(dk, n1)
        qkvg_s[V_ROWS, :] += dot_nn(dv, n1)
        back_t = dot_nn(w_ref[:, Q_ROWS], dq) + dot_nn(w_ref[:, K_ROWS], dk) + dot_nn(w_ref[:, V_ROWS], dv)
        back_s[i] = back_t.T
    gain_total = jnp.zeros((8, D), f32)
    shift_total = jnp.zeros((8, D), f32)
    for i in range(images):
        for block in blocks(LP):
            scaled, inv_std = scaled_s[i, block, :], inv_s[i, block, :]
            back = masked(back_s[i, block, :], tokens)
            gain_total = gain_total + fold_rows(back * scaled)
            shift_total = shift_total + fold_rows(back)
            ing_ref[i, 0, block, :] = resg_ref[0, i * LP + block.start : i * LP + block.stop, :] + norm_backward(
                back, scaled, inv_std, g1_ref[...], keep, inv_active
            )
    norm_s[0:1, :] += rows_sum(gain_total)
    norm_s[1:2, :] += rows_sum(shift_total) * keep

    @pl.when(member == SUBNETS - 1)
    def _():
        proj = dot_nt(projg_s[...].T.astype(bf16), pick_heads_ref[...])
        pieces = [(0, 0, D), (D, 256, HALF), (PAIR, 256 + HALF, HALF)]
        pieces += [(PAIR + HALF + h * E, 512 + h * EP, E) for h in range(H)]
        for to, at, size in pieces:
            grads_s[to : to + size, :] = qkvg_s[at : at + size, :]
        grads_s[QKV_HALF:PAIR, :] = proj[:HALF]
        grads_s[PAIR + QKV_HALF :, :] = proj[HALF:]
        mine_ref[...] = grads_s[pl.ds(pl.multiple_of(place[1] * PAIR, 16), PAIR), :].astype(bf16)
        send_ref[...] = grads_s[pl.ds(pl.multiple_of((1 - place[1]) * PAIR, 16), PAIR), :].astype(bf16)
        small_ref[...] = jnp.zeros_like(small_ref)
        for k in range(2):
            small_ref[2 * k : 2 * k + 1, :] = norm_s[k : k + 1, :HALF]
            small_ref[2 * k + 1 : 2 * k + 2, :] = norm_s[k : k + 1, HALF:]
        talk = jnp.concatenate([rows_sum(talk_s[h]) for h in range(H)], axis=0) * HEAD_SCALE
        small_ref[4 : 4 + H, :H] = lax.dot_general(
            talk, head_lanes(), (((1,), (1,)), ((), ())), precision=lax.Precision.HIGHEST, preferred_element_type=f32
        )


def finish_kernel(
    attend_ref, tail_ref, ff_ref, small_ref, totals2_ref,
    qkv_ref, proj_ref, fc1_ref, fc2_ref, n1g_ref, n1s_ref, pb_ref, n2g_ref, n2s_ref, ob_ref, taps_ref, gain_ref, shift_ref,
    talk_ref,
):
    qkv_ref[...] = attend_ref[:QKV_HALF, :].astype(f32)
    proj_ref[...] = attend_ref[QKV_HALF:, :].astype(f32).T
    fc1_ref[...] = ff_ref[: FF // 2, :].astype(f32)
    fc2_ref[...] = ff_ref[FF // 2 :, :].astype(f32)
    taps_rows = 9 * FF // HALF
    vectors = [(n1g_ref, tail_ref, 0), (n1s_ref, tail_ref, 2)]
    vectors += [(ref, small_ref, taps_rows + 2 * k) for k, ref in enumerate((n2g_ref, n2s_ref, pb_ref, ob_ref))]
    for ref, source, row in vectors:
        for part in range(2):
            ref[part * HALF : (part + 1) * HALF] = source[row + part, :]
    for k in range(FF // HALF):
        taps_ref[:, k * HALF : (k + 1) * HALF] = small_ref[pl.ds(k, 9, stride=FF // HALF), :]
    total = sum(totals2_ref[s] for s in range(SUBNETS))
    shift_ref[...] = total[0]
    gain_ref[...] = total[1]
    talk_ref[...] = tail_ref[4 : 4 + H, :H]


def whole(shape):
    return pl.BlockSpec(shape, lambda s: (0,) * len(shape))


def per_member(shape):
    return pl.BlockSpec((1,) + shape, lambda s: (s,) + (0,) * len(shape))


def per_image(images):
    return pl.BlockSpec((images, 1, LP, D), lambda s: (0, s, 0, 0))


SMEM = pl.BlockSpec(memory_space=pltpu.SMEM)


def sds(shape, dtype=f32):
    return jax.ShapeDtypeStruct(shape, dtype)


KEPT = pl.BlockSpec(memory_space=pltpu.VMEM)


def keep_near(*arrays):
    return tuple(pltpu.with_memory_space_constraint(v, pltpu.VMEM) for v in arrays)


def params():
    return pltpu.CompilerParams(vmem_limit_bytes=56 * MIB, dimension_semantics=("arbitrary",))


def cost(microseconds, moved):
    return pl.CostEstimate(flops=int(microseconds * 5e8), bytes_accessed=moved, transcendentals=0)


def swap(value, axis, step=1):
    size = lax.axis_size(axis)
    return lax.ppermute(value, axis, [(i, i ^ step) for i in range(size)])


def steps_of(axis):
    step, size = 1, lax.axis_size(axis)
    while step < size:
        yield step
        step *= 2


def add_low(a, b):
    return (a.astype(f32) + b.astype(f32)).astype(bf16)


def sum_over(value, axes):
    for axis in axes:
        for step in steps_of(axis):
            value = value + swap(value, axis, step)
    return value


def split_pair(value):
    high = value.astype(bf16)
    return high, (value - high.astype(f32)).astype(bf16)


def halves(value, dim, mine):
    low, high = jnp.split(value, 2, axis=dim)
    return jnp.where(mine == 0, low, high), jnp.where(mine == 0, high, low)


def exchange_packed(send, keep, small, axis, step):
    rows, extra = send.shape[0], small.shape[0]
    got = swap(jnp.concatenate((send,) + split_pair(small), axis=0), axis, step)
    return (
        add_low(keep, got[:rows]),
        small + (got[rows : rows + extra].astype(f32) + got[rows + extra :].astype(f32)),
    )


def sum_packed(big, small, axes):
    for axis in axes:
        for step in steps_of(axis):
            big, small = exchange_packed(big, big, small, axis, step)
    return big, small


def tie(*values):
    return lax.optimization_barrier(values)


def in_order(mine, first, second, dim):
    return jnp.where(mine == 0, jnp.concatenate([first, second], dim), jnp.concatenate([second, first], dim))


def to_grid(flat):
    return flat.reshape(flat.shape[0], SUBNETS, GRID, GRID, D)


def to_tokens(grid):
    images = grid.shape[0]
    grid = jnp.pad(grid, ((0, 0), (0, 0), (0, 0), (0, COLS - GRID), (0, 0)))
    return grid.reshape(images, SUBNETS, LP, D)


def from_tokens(tokens):
    images = tokens.shape[0]
    grid = tokens.reshape(images, SUBNETS, GRID, COLS, D)[:, :, :, :GRID]
    return grid.reshape(images, SUBNETS * L * D)


def pad_to(value, axis, size):
    widths = [(0, 0)] * value.ndim
    widths[axis] = (0, size - value.shape[axis])
    return jnp.pad(value, widths)


def one_hot(rows, cols, pairs):
    out = np.zeros((rows, cols), np.float32)
    for r, c in pairs:
        out[r, c] = 1.0
    return out


PLACE = np.stack([one_hot(D, HALF, [(c * HALF + j, j) for j in range(HALF)]) for c in range(2)])
PICK_HEADS = one_hot(D, VP, [(j, j // E * EP + j % E) for j in range(D)])


def weight_kernel(
    place, a_ref, b_ref, c_ref, d_ref, place_ref, w_ref, wt_ref, proj_ref, fc1_ref, full_s, heads_s,
):
    row, col = place[0], place[1]

    def spread(first, second, index, rows):
        return dot_nt(first[rows, :], place_ref[index]) + dot_nt(second[rows, :], place_ref[1 - index])

    qkv_rows, proj_rows = slice(0, QKV_HALF), slice(QKV_HALF, PAIR)
    mine, other = spread(a_ref, b_ref, row, qkv_rows), spread(c_ref, d_ref, row, qkv_rows)
    low, high = jnp.where(col == 0, mine, other), jnp.where(col == 0, other, mine)
    full_s[...] = jnp.zeros_like(full_s)
    full_s[:D, :] = low[:D]
    full_s[256 : 256 + HALF, :] = low[D:]
    full_s[256 + HALF : 256 + D, :] = high[:HALF]
    for h in range(H):
        full_s[512 + h * EP : 512 + h * EP + E, :] = high[HALF + h * E : HALF + h * E + E]
    wt_ref[...] = full_s[...].astype(bf16)
    w_ref[...] = full_s[...].T.astype(bf16)
    mine, other = spread(a_ref, c_ref, col, proj_rows), spread(b_ref, d_ref, col, proj_rows)
    parts = jnp.where(row == 0, mine, other), jnp.where(row == 0, other, mine)
    heads_s[...] = jnp.zeros_like(heads_s)
    for h in range(H):
        first = h % (H // 2) * E
        heads_s[h * EP : h * EP + E, :] = parts[h // (H // 2)][first : first + E]
    proj_ref[...] = heads_s[...].astype(bf16)
    fc1_rows = slice(PAIR, PAIR + FF // 2)
    mine = spread(a_ref, b_ref, row, fc1_rows).astype(bf16)
    other = spread(c_ref, d_ref, row, fc1_rows).astype(bf16)
    fc1_ref[: FF // 2, :] = jnp.where(col == 0, mine, other)
    fc1_ref[FF // 2 :, :] = jnp.where(col == 0, other, mine)


def body(
    block_in, out_grad, width_mask, head_mask, hidden_mask, qkv_weight, proj_weight, fc1_weight, fc2_weight,
    norm1_gain, norm1_shift, proj_bias, norm2_gain, second_norm_bias, conv_taps, bn_gain, bn_shift, output_bias,
    talk_mix,
):
    images = block_in.shape[0]
    rows = images * LP
    devices_all = lax.axis_size("dp") * lax.axis_size("row") * lax.axis_size("col")
    tokens_all = float(devices_all * images * L)
    row, col = lax.axis_index("row"), lax.axis_index("col")

    place = jnp.stack([row, col])

    front_own = jnp.concatenate([qkv_weight.T, proj_weight, fc1_weight.T], axis=0)
    front_row, x, place = tie(swap(front_own, "row"), to_tokens(to_grid(block_in)), place)
    front_col, front_both = swap(front_own, "col"), swap(front_row, "col")

    w, wt, proj, fc1 = pl.pallas_call(
        weight_kernel,
        in_specs=[SMEM] + [KEPT] * 5,
        out_specs=[KEPT] * 4,
        out_shape=[sds((D, WP), bf16), sds((WP, D), bf16), sds((VP, D), bf16), sds((FF, D), bf16)],
        scratch_shapes=[pltpu.VMEM((WP, D), f32), pltpu.VMEM((VP, D), f32)],
        name="weights",
    )(
        place, *keep_near(front_own, front_row, front_col, front_both), jnp.asarray(PLACE, bf16),
    )
    fc2_own, wt = tie(fc2_weight, wt)
    fc2_row = swap(fc2_own, "row")
    fc2_col, fc2_both = swap(fc2_own, "col"), swap(fc2_row, "col")
    fc2 = in_order(row, in_order(col, fc2_own, fc2_col, 1), in_order(col, fc2_row, fc2_both, 1), 0)

    g1, b1, pb, g2, b2, ob = (
        v[None] for v in (norm1_gain, norm1_shift, proj_bias, norm2_gain, second_norm_bias, output_bias)
    )
    gain, shift = bn_gain[None], bn_shift[None]

    og = to_tokens(to_grid(out_grad))

    row_spec = per_member((rows, D))
    wide_spec = per_member((rows, FF))
    e_spec = per_member((images, H, LP, LP))
    inv_spec = per_member((images, H, LP))
    att_spec = per_member((images, VP, LP))
    width_spec, head_spec, hidden_spec, talk_spec = (whole(v) for v in ((SUBNETS, D), (SUBNETS, H), (SUBNETS, FF), (H, H)))
    vec, wide_vec, taps_spec = whole((1, D)), whole((1, FF)), whole((9, FF))
    w_spec, wt_spec, proj_spec = whole((D, WP)), whole((WP, D)), whole((VP, D))
    halo = pltpu.VMEM((2, 2, EDGE + images * HALO + EDGE, 128), f32)

    e, inv, att, res, hid, conv, sums = pl.pallas_call(
        functools.partial(front_kernel, images),
        grid=(SUBNETS,),
        in_specs=[
            SMEM, SMEM, per_image(images), width_spec, head_spec, hidden_spec, talk_spec, vec, vec, wt_spec, w_spec,
            proj_spec, vec, vec, vec, whole((FF, D)), taps_spec,
        ],
        out_specs=[e_spec, inv_spec, att_spec, row_spec, wide_spec, wide_spec, KEPT],
        out_shape=[
            sds((SUBNETS, images, H, LP, LP), bf16), sds((SUBNETS, images, H, LP)), sds((SUBNETS, images, VP, LP), bf16),
            sds((SUBNETS, rows, D)), sds((SUBNETS, rows, FF), bf16), sds((SUBNETS, rows, FF)),
            pltpu.VMEM((SUBNETS, 2, FF), f32),
        ],
        scratch_shapes=[
            pltpu.VMEM((images, LP, D), bf16), pltpu.VMEM((images, CP, LP), bf16), pltpu.VMEM((images, LP, CP), f32),
            pltpu.VMEM((images, VP, LP), bf16), pltpu.VMEM((SLOTS, LP, LP), f32), pltpu.VMEM((H, CP), f32),
            pltpu.VMEM((rows, D), bf16), halo,
        ],
        compiler_params=params(),
        cost_estimate=cost(30, 40 * MIB),
        name="front",
    )(
        head_mask, hidden_mask, x, width_mask, head_mask, hidden_mask, talk_mix, g1, b1, wt, w, proj, pb, g2, b2, fc1,
        conv_taps,
    )

    totals = sum_over(sums, ("col", "row", "dp"))

    block_out, ng, sums2, fc2_keep, fc2_send, out_bias_grad, bn_mean, bn_var = pl.pallas_call(
        functools.partial(middle_kernel, images, tokens_all),
        grid=(SUBNETS,),
        in_specs=[
            SMEM, SMEM, wide_spec, row_spec, per_image(images), width_spec, hidden_spec, whole((FF, D)), vec,
            wide_vec, wide_vec, KEPT,
        ],
        out_specs=[
            per_image(images), wide_spec, KEPT, KEPT, KEPT, vec, hidden_spec, hidden_spec,
        ],
        out_shape=[
            sds((images, SUBNETS, LP, D)), sds((SUBNETS, rows, FF), bf16), pltpu.VMEM((SUBNETS, 2, FF), f32),
            pltpu.VMEM((FF, HALF), bf16), pltpu.VMEM((FF, HALF), bf16), sds((1, D)), sds((SUBNETS, FF)), sds((SUBNETS, FF)),
        ],
        scratch_shapes=[
            pltpu.VMEM((rows, D), bf16), pltpu.VMEM((rows, D), f32), pltpu.VMEM((2, rows, CHUNK), bf16),
            pltpu.VMEM((2, rows, CHUNK), f32), pltpu.VMEM((D, FF), f32),
        ],
        compiler_params=params(),
        cost_estimate=cost(12, 26 * MIB),
        name="middle",
    )(hidden_mask, place, conv, res, og, width_mask, hidden_mask, fc2, ob, gain, shift, *keep_near(totals))

    totals2 = sum_over(sums2, ("col", "row", "dp"))
    fc2_keep, fc2_send = halves(add_low(fc2_keep, swap(fc2_send, "col")), 0, row)
    fc2_part = add_low(fc2_keep, swap(fc2_send, "row"))
    totals2, fc2_part = tie(totals2, fc2_part)

    res_grad, fc1_keep, fc1_send, small = pl.pallas_call(
        functools.partial(hidden_back_kernel, images, tokens_all),
        grid=(SUBNETS,),
        in_specs=[
            SMEM, SMEM, vec, per_image(images), row_spec, wide_spec, wide_spec, wide_spec, width_spec, vec, vec,
            whole((FF, D)), taps_spec, wide_vec, KEPT, KEPT,
        ],
        out_specs=[row_spec, KEPT, KEPT, KEPT],
        out_shape=[
            sds((SUBNETS, rows, D)), pltpu.VMEM((FF // 2, D), bf16), pltpu.VMEM((FF // 2, D), bf16),
            pltpu.VMEM((SMALL, HALF), f32),
        ],
        scratch_shapes=[
            halo, pltpu.VMEM((rows, D), f32), pltpu.VMEM((rows, D), bf16), pltpu.VMEM((2, rows, CHUNK), bf16),
            pltpu.VMEM((D, FF), f32), pltpu.VMEM((FF, D), bf16), pltpu.VMEM((9, FF), f32), pltpu.VMEM((8, D), f32),
            pltpu.VMEM((rows, D), f32), pltpu.VMEM((rows, 1), f32),
        ],
        compiler_params=params(),
        cost_estimate=cost(25, 31 * MIB),
        name="hidden_back",
    )(hidden_mask, place, out_bias_grad, og, res, hid, conv, ng, width_mask, g2, b2, fc1, conv_taps, gain, *keep_near(totals, totals2))

    small = small + swap(small, "col")
    fc1_keep, fc1_send = halves(add_low(fc1_keep, swap(fc1_send, "col")), 1, row)
    block_out, fc1_send = tie(block_out, fc1_send)
    block_out = from_tokens(block_out)
    fc1_part, small = exchange_packed(fc1_send, fc1_keep, small, "row", 1)
    ff_grads = jnp.concatenate([fc1_part, fc2_part])
    dp_steps = list(steps_of("dp"))
    far_first = dp_steps[::-1]
    ff_grads, block_out, res_grad = tie(ff_grads, block_out, res_grad)
    ff_grads, small = exchange_packed(ff_grads, ff_grads, small, "dp", far_first[0])

    in_grad, mine, send, tail = pl.pallas_call(
        functools.partial(attend_back_kernel, images),
        grid=(SUBNETS,),
        in_specs=[
            SMEM, SMEM, per_image(images), row_spec, e_spec, inv_spec, att_spec, width_spec, head_spec, talk_spec, vec, vec,
            wt_spec, w_spec, proj_spec, whole((D, VP)),
        ],
        out_specs=[per_image(images), KEPT, KEPT, KEPT],
        out_shape=[
            sds((images, SUBNETS, LP, D)), pltpu.VMEM((PAIR, D), bf16), pltpu.VMEM((PAIR, D), bf16),
            pltpu.VMEM((16, HALF), f32),
        ],
        scratch_shapes=[
            pltpu.VMEM((H, 8, CP), f32),
            pltpu.VMEM((8, D), f32),
            pltpu.VMEM((2 * PAIR, D), f32),
            pltpu.VMEM((VP, D), f32),
            pltpu.VMEM((WP, D), f32),
            pltpu.VMEM((images, LP, D), bf16),
            pltpu.VMEM((images, LP, D), bf16),
            pltpu.VMEM((images, LP, CP), bf16),
            pltpu.VMEM((images, LP, CP), f32),
            pltpu.VMEM((images, CP, LP), bf16),
            pltpu.VMEM((images, LP, VP), bf16),
            pltpu.VMEM((H, CP), f32),
            pltpu.VMEM((H, CP, 128), f32),
            pltpu.VMEM((images, VP, LP), f32),
            pltpu.VMEM((images, CP, LP), f32),
            pltpu.VMEM((images, LP, CP), f32),
            pltpu.VMEM((images, VP, LP), f32),
            pltpu.VMEM((SLOTS, 2, EP, LP), bf16),
            pltpu.VMEM((SLOTS, 2, LP, LP), f32),
            pltpu.VMEM((SLOTS, 2, LP, LP), bf16),
            pltpu.VMEM((images, LP, D), f32),
            pltpu.VMEM((images, LP, D), f32),
            pltpu.VMEM((images, LP, 1), f32),
        ],
        compiler_params=params(),
        cost_estimate=cost(33, 32 * MIB),
        name="attend_back",
    )(
        head_mask, place, x, res_grad, e, inv, att, width_mask, head_mask, talk_mix, g1, b1, wt, w, proj,
        jnp.asarray(PICK_HEADS, bf16),
    )

    mine, send, tail, in_grad, ff_grads, small = tie(mine, send, tail, in_grad, ff_grads, small)
    if len(dp_steps) > 1:
        ff_grads, small = exchange_packed(ff_grads, ff_grads, small, "dp", far_first[1])
    tail = tail + swap(tail, "col")
    keep, send = halves(add_low(mine, swap(send, "col")), 1, row)
    attend_grads, tail = exchange_packed(send, keep, tail, "row", 1)
    for n, step in enumerate(dp_steps[1:2] + dp_steps[:1] + dp_steps[2:]):
        if n + 2 < len(dp_steps):
            ff_grads, small = exchange_packed(ff_grads, ff_grads, small, "dp", far_first[n + 2])
        if n + 1 == len(dp_steps):
            in_grad, attend_grads = tie(in_grad, attend_grads)
            in_grad = from_tokens(in_grad)
        attend_grads, tail = exchange_packed(attend_grads, attend_grads, tail, "dp", step)

    qkvg, projg, fc1g, fc2g, n1g, n1s, pbg, n2g, n2s, obg, tapsg, bng, bns, talkg = pl.pallas_call(
        finish_kernel,
        in_specs=[KEPT] * 5,
        out_shape=[
            sds((QKV_HALF, HALF)), sds((HALF, HALF)), sds((FF // 2, HALF)), sds((FF // 2, HALF)),
            *(sds((D,)) for _ in range(6)), sds((9, FF)), sds((FF,)), sds((FF,)), sds((H, H)),
        ],
        name="finish",
    )(*keep_near(attend_grads, tail, ff_grads, small, totals2))
    return (
        block_out, in_grad, qkvg.T, projg, fc1g.T, fc2g, n1g, n1s, pbg, n2g, n2s, tapsg, bng, bns, obg, talkg, bn_mean,
        bn_var,
    )


def solution(mesh):
    split = P(AXES, None)
    weight = P("row", "col")
    in_specs = (split, split, P(), P(), P()) + (weight,) * 4 + (P(),) * 10
    out_specs = (split, split) + (weight,) * 4 + (P(),) * 12
    return jax.shard_map(body, mesh=mesh, in_specs=in_specs, out_specs=out_specs, check_vma=False)
```
